32 devices in a mesh: fsdp: 8 (over y, x, core), tp: 4 (over z).
Axes of the slice: x: 2, y: 2, z: 4, core: 2. Of those that a mesh axis runs over, the one named last changes fastest.
Arguments:
- tokens: bfloat16 [16, 8192], P('fsdp', 'tp'), may hold values from -6 to 6
- gate_weight: bfloat16 [27648, 8192], P('fsdp', 'tp'), may hold values from -0.0625 to 0.0625
- up_weight: bfloat16 [27648, 8192], P('fsdp', 'tp'), may hold values from -0.0625 to 0.0625
- down_weight: bfloat16 [27648, 8192], P('fsdp', 'tp'), may hold values from -0.0390625 to 0.0390625
Outputs:
- mixed: bfloat16 [16, 8192], P('fsdp', 'tp')
The draws below stay inside these ranges and needn't reach their ends.
All inputs are finite; a program needn't handle non-finite values.
Results may differ from the reference program's by a relative error of at most 0.0049.
Values may be sent and summed in bfloat16 or wider, within the bound.
A program may use at most 128 MiB of HBM per device.

```python
import jax
import jax.numpy as jnp

D = 8192
FF = 27648
TOKENS = 16


def block_levels(key, shape, shards, least, high):
    gain, own = 1.0, jax.random.fold_in(key, 6)
    for axis_at, shards_of in shards:
        steps = jnp.exp(jax.random.uniform(jax.random.fold_in(own, axis_at), (shards_of,), jnp.float32, least / len(shards), high / len(shards)))
        gain = gain * jnp.repeat(steps, shape[axis_at] // shards_of).reshape([-1 if axis == axis_at else 1 for axis in range(len(shape))])
    return gain


def centred(stream_key, extent, deviation, limit, pieces=(), held_as=jnp.bfloat16):
    entries = jax.random.normal(stream_key, extent, jnp.float32) * deviation
    if len(pieces) > 0:
        entries = block_levels(stream_key, extent, pieces, -0.22, 0.18) * entries
    return jnp.clip(entries, min=-limit, max=limit).astype(held_as)


def setup_inputs(seed: int = 0) -> dict:
    streams_of = jax.random.split(jax.random.key(seed), 5)
    tokens = centred(streams_of[0], (TOKENS, D), 1.0, 6.0, ((0, 8), (1, 4)))
    gate_weight = centred(streams_of[1], (FF, D), D ** -0.5, 0.0625, ((0, 8), (1, 4)))
    up_weight = centred(streams_of[2], (FF, D), D ** -0.5, 0.0625, ((0, 8), (1, 4)))
    down_weight = centred(streams_of[3], (FF, D), FF ** -0.5, 0.0390625, ((0, 8), (1, 4)))
    return {"tokens": tokens, "gate_weight": gate_weight, "up_weight": up_weight, "down_weight": down_weight}


def reference(tokens, gate_weight, up_weight, down_weight):
    gate = jnp.dot(tokens, gate_weight.T, preferred_element_type=jnp.float32)
    up = jnp.dot(tokens, up_weight.T, preferred_element_type=jnp.float32)
    hidden = (jax.nn.silu(gate) * up).astype(jnp.bfloat16)
    mixed = jnp.dot(hidden, down_weight, preferred_element_type=jnp.float32)
    return mixed.astype(jnp.bfloat16)
```

```python
import functools

import jax
import jax.numpy as jnp
from jax import lax
from jax.experimental import pallas as pl
from jax.experimental.pallas import tpu as pltpu
from jax.sharding import PartitionSpec as P

MESH = pl.DeviceIdType.MESH
GROUP = 128
LAG = 2
WIRE = jnp.float32
NT = (((1,), (1,)), ((), ()))
VMEM_BYTES = 58 * 2**20


def fused(n_fsdp, n_tp, tokens, gate_w, up_w, down_w, out,
          wg, wu, wd, slots, xf, x, part, own, recv, hid, acc, send, land,
          w_sem, own_sem, tok_send, tok_recv, p_send, p_recv, h_send, h_recv, o_send, o_recv):
    f, t = lax.axis_index("fsdp"), lax.axis_index("tp")
    rows, hidden = tokens.shape[0], gate_w.shape[0]
    chunk = GROUP * n_tp
    n_chunks = -(-hidden // chunk)
    full = hidden // chunk
    last_owners = (hidden - full * chunk) // GROUP

    def width(s):
        return min(chunk, hidden - s * chunk)

    def load(k, source, target, s):
        at = pl.ds(s * chunk, width(s))
        return pltpu.make_async_copy(source.at[at], target.at[at], w_sem.at[k, s])

    for s in range(n_chunks):
        load(0, gate_w, wg, s).start()
        load(1, up_w, wu, s).start()
    for s in range(n_chunks):
        load(2, down_w, wd, s).start()

    own_copy = pltpu.make_async_copy(tokens, slots.at[f], own_sem)
    own_copy.start()

    barrier = pltpu.get_barrier_semaphore()
    for d in range(1, n_fsdp):
        pl.semaphore_signal(barrier, inc=1, device_id={"fsdp": lax.rem(f + d, n_fsdp)}, device_id_type=MESH)
    for d in range(1, n_tp):
        pl.semaphore_signal(barrier, inc=1, device_id={"tp": lax.rem(t + d, n_tp)}, device_id_type=MESH)
    pl.semaphore_wait(barrier, n_fsdp + n_tp - 2)

    def tok_copy(d, slot, peer):
        return pltpu.make_async_remote_copy(
            tokens, slots.at[slot], tok_send.at[d - 1], tok_recv.at[d - 1],
            device_id={"fsdp": peer}, device_id_type=MESH)

    for d in range(1, n_fsdp):
        tok_copy(d, f, lax.rem(f + d, n_fsdp)).start()
    own_copy.wait()
    for d in range(1, n_fsdp):
        tok_copy(d, lax.rem(f + n_fsdp - d, n_fsdp), f).wait_recv()
    for p in range(n_fsdp):
        xf[p * rows:(p + 1) * rows, :] = slots[p].astype(jnp.float32)
    x[...] = xf[...].astype(x.dtype)
    acc[...] = jnp.zeros_like(acc)

    def when(cond, run):
        if cond is True:
            run()
        else:
            pl.when(cond)(run)

    def part_copy(s, d):
        peer = lax.rem(t + d, n_tp)
        return pltpu.make_async_remote_copy(
            part.at[s, peer], recv.at[s, d - 1], p_send.at[s, d - 1], p_recv.at[s, d - 1],
            device_id={"tp": peer}, device_id_type=MESH)

    def hid_copy(s, d, owner):
        return pltpu.make_async_remote_copy(
            hid.at[s, owner], hid.at[s, owner], h_send.at[s, d - 1], h_recv.at[s, d - 1],
            device_id={"tp": lax.rem(t + d, n_tp)}, device_id_type=MESH)

    def gate_up(s, owners):
        size = owners * GROUP
        at = pl.ds(pl.multiple_of(s * chunk, chunk), size)
        for k, (source, target) in enumerate(((gate_w, wg), (up_w, wu))):
            pltpu.make_async_copy(source.at[at], target.at[at], w_sem.at[k, s]).wait()
            sums = lax.dot_general(x[...], target[at, :], NT, preferred_element_type=jnp.float32)
            for j in range(owners):
                piece = sums[:, j * GROUP:(j + 1) * GROUP]
                part[s, j, k] = piece.astype(part.dtype)

                @pl.when(t == j)
                def _():
                    own[s, k] = piece
        for d in range(1, n_tp):
            when(True if owners == n_tp else lax.rem(t + d, n_tp) < owners,
                 lambda d=d: part_copy(s, d).start())

    def activate(s, owners):
        def run():
            gate, up = own[s, 0], own[s, 1]
            for d in range(1, n_tp):
                part_copy(s, d).wait_recv()
                gate = gate + recv[s, d - 1, 0].astype(jnp.float32)
                up = up + recv[s, d - 1, 1].astype(jnp.float32)
            hid[s, t] = (gate / (1.0 + jnp.exp(-gate)) * up).astype(hid.dtype)
            for d in range(1, n_tp):
                hid_copy(s, d, t).start()
        when(True if owners == n_tp else t < owners, run)

    def down(s, owners):
        size = owners * GROUP
        at = pl.ds(pl.multiple_of(s * chunk, chunk), size)
        for d in range(1, n_tp):
            owner = lax.rem(t + n_tp - d, n_tp)
            when(True if owners == n_tp else owner < owners,
                 lambda d=d, owner=owner: hid_copy(s, d, owner).wait_recv())
        pltpu.make_async_copy(down_w.at[at], wd.at[at], w_sem.at[2, s]).wait()
        h = jnp.concatenate([hid[s, j] for j in range(owners)], axis=1)
        acc[...] += jnp.dot(h, wd[at, :], preferred_element_type=jnp.float32)

    @pl.loop(0, full)
    def _(s):
        gate_up(s, n_tp)

        @pl.when(s >= LAG)
        def _():
            activate(s - LAG, n_tp)

    if last_owners:
        gate_up(full, last_owners)

    @pl.loop(full - LAG, full)
    def _(s):
        activate(s, n_tp)

    early = min(2, full)

    @pl.loop(0, early)
    def _(s):
        down(s, n_tp)

    if last_owners:
        activate(full, last_owners)

    @pl.loop(early, full)
    def _(s):
        down(s, n_tp)

    if last_owners:
        down(full, last_owners)

    def out_copy(d, peer):
        return pltpu.make_async_remote_copy(
            send.at[peer], land.at[d - 1], o_send.at[d - 1], o_recv.at[d - 1],
            device_id={"fsdp": peer}, device_id_type=MESH)

    for p in range(n_fsdp):
        send[p] = acc[p * rows:(p + 1) * rows, :]
    for d in range(1, n_fsdp):
        out_copy(d, lax.rem(f + d, n_fsdp)).start()
    total = send[f]
    for d in range(1, n_fsdp):
        out_copy(d, f).wait_recv()
        total = total + land[d - 1]
    out[...] = total.astype(out.dtype)

    for d in range(1, n_fsdp):
        tok_copy(d, f, f).wait_send()
        out_copy(d, f).wait_send()

    @pl.loop(0, full)
    def _(s):
        for d in range(1, n_tp):
            part_copy(s, d).wait_send()
            hid_copy(s, d, t).wait_send()

    if last_owners:
        for d in range(1, n_tp):
            when(lax.rem(t + d, n_tp) < last_owners, lambda d=d: part_copy(full, d).wait_send())
            when(t < last_owners, lambda d=d: hid_copy(full, d, t).wait_send())


def fused_call(n_fsdp, n_tp, tokens, gate_w, up_w, down_w):
    rows, width = tokens.shape
    hidden = gate_w.shape[0]
    chunks = -(-hidden // (GROUP * n_tp))
    every = rows * n_fsdp
    dma = pltpu.SemaphoreType.DMA
    any_spec = pl.BlockSpec(memory_space=pl.ANY)
    return pl.pallas_call(
        functools.partial(fused, n_fsdp, n_tp),
        out_shape=jax.ShapeDtypeStruct((rows, width), tokens.dtype),
        in_specs=[any_spec] * 4,
        out_specs=pl.BlockSpec(memory_space=pltpu.VMEM),
        scratch_shapes=[
            pltpu.VMEM((hidden, width), gate_w.dtype),
            pltpu.VMEM((hidden, width), up_w.dtype),
            pltpu.VMEM((hidden, width), down_w.dtype),
            pltpu.VMEM((n_fsdp, rows, width), tokens.dtype),
            pltpu.VMEM((every, width), jnp.float32),
            pltpu.VMEM((every, width), tokens.dtype),
            pltpu.VMEM((chunks, n_tp, 2, every, GROUP), WIRE),
            pltpu.VMEM((chunks, 2, every, GROUP), jnp.float32),
            pltpu.VMEM((chunks, n_tp - 1, 2, every, GROUP), WIRE),
            pltpu.VMEM((chunks, n_tp, every, GROUP), jnp.bfloat16),
            pltpu.VMEM((every, width), jnp.float32),
            pltpu.VMEM((n_fsdp, rows, width), jnp.float32),
            pltpu.VMEM((n_fsdp - 1, rows, width), jnp.float32),
            dma((3, chunks)),
            dma,
            dma((n_fsdp - 1,)),
            dma((n_fsdp - 1,)),
            dma((chunks, n_tp - 1)),
            dma((chunks, n_tp - 1)),
            dma((chunks, n_tp - 1)),
            dma((chunks, n_tp - 1)),
            dma((n_fsdp - 1,)),
            dma((n_fsdp - 1,)),
        ],
        compiler_params=pltpu.CompilerParams(
            collective_id=0, has_side_effects=True, vmem_limit_bytes=VMEM_BYTES),
        cost_estimate=pl.CostEstimate(
            flops=6 * every * hidden * width, bytes_accessed=6 * hidden * width,
            transcendentals=every * hidden // n_tp),
        name="swiglu",
    )(tokens, gate_w, up_w, down_w)


def collective_body(tokens, gate_weight, up_weight, down_weight):
    hidden_width = gate_weight.shape[0]
    block_rows = lax.all_gather(tokens, "fsdp", axis=0, tiled=True)
    gate_part = lax.dot_general(block_rows, gate_weight, NT, preferred_element_type=jnp.float32)
    up_part = lax.dot_general(block_rows, up_weight, NT, preferred_element_type=jnp.float32)
    partial_value = jnp.concatenate([gate_part, up_part], axis=1)
    share_rows = lax.psum_scatter(partial_value, "tp", scatter_dimension=0, tiled=True)
    quarter = (jax.nn.silu(share_rows[:, :hidden_width]) * share_rows[:, hidden_width:]).astype(
        jnp.bfloat16
    )
    hidden = lax.all_gather(quarter, "tp", axis=0, tiled=True)
    down_terms = jnp.dot(hidden, down_weight, preferred_element_type=jnp.float32)
    mixed = lax.psum_scatter(down_terms, "fsdp", scatter_dimension=0, tiled=True)
    return mixed.astype(jnp.bfloat16)


def solution(mesh):
    n_fsdp, n_tp = mesh.shape["fsdp"], mesh.shape["tp"]

    def body(tokens, gate_weight, up_weight, down_weight):
        hidden, width = gate_weight.shape
        every = tokens.shape[0] * n_fsdp
        resident = 6 * hidden * width + 24 * every * width + 48 * every * hidden
        if hidden % GROUP or hidden < GROUP * n_tp * LAG or every % 16 or resident > VMEM_BYTES:
            return collective_body(tokens, gate_weight, up_weight, down_weight)
        return fused_call(n_fsdp, n_tp, tokens, gate_weight, up_weight, down_weight)

    placed = (P("fsdp", "tp"),) * 4
    return jax.shard_map(
        body, mesh=mesh, in_specs=placed, out_specs=P("fsdp", "tp"), check_vma=False
    )
```

```python
import functools

import jax
import jax.numpy as jnp
from jax import lax
from jax.experimental import pallas as pl
from jax.experimental.pallas import tpu as pltpu
from jax.sharding import PartitionSpec as P

MESH = pl.DeviceIdType.MESH
GROUP = 128
LAG = 2
WIRE = jnp.float32
NT = (((1,), (1,)), ((), ()))
VMEM_BYTES = 58 * 2**20


def fused(n_fsdp, n_tp, tokens, gate_w, up_w, down_w, out,
          wg, wu, wd, slots, xf, x, part, own, recv, hid, acc, send, land,
          w_sem, own_sem, tok_send, tok_recv, p_send, p_recv, h_send, h_recv, o_send, o_recv):
    f, t = lax.axis_index("fsdp"), lax.axis_index("tp")
    rows, hidden = tokens.shape[0], gate_w.shape[0]
    chunk = GROUP * n_tp
    n_chunks = -(-hidden // chunk)
    full = hidden // chunk
    last_owners = (hidden - full * chunk) // GROUP

    def width(s):
        return min(chunk, hidden - s * chunk)

    def load(k, source, target, s):
        size = chunk if not isinstance(s, int) else width(s)
        at = pl.ds(s * chunk if isinstance(s, int) else pl.multiple_of(s * chunk, chunk), size)
        return pltpu.make_async_copy(source.at[at], target.at[at], w_sem.at[k, s])

    def load_gate_up(s):
        load(0, gate_w, wg, s).start()
        load(1, up_w, wu, s).start()

    def load_down(s):
        load(2, down_w, wd, s).start()

    load_gate_up(0)
    own_copy = pltpu.make_async_copy(tokens, slots.at[f], own_sem)
    own_copy.start()

    barrier = pltpu.get_barrier_semaphore()
    for d in range(1, n_fsdp):
        pl.semaphore_signal(barrier, inc=1, device_id={"fsdp": lax.rem(f + d, n_fsdp)}, device_id_type=MESH)
    for d in range(1, n_tp):
        pl.semaphore_signal(barrier, inc=1, device_id={"tp": lax.rem(t + d, n_tp)}, device_id_type=MESH)
    pl.semaphore_wait(barrier, n_fsdp + n_tp - 2)

    def tok_copy(d, slot, peer):
        return pltpu.make_async_remote_copy(
            tokens, slots.at[slot], tok_send.at[d - 1], tok_recv.at[d - 1],
            device_id={"fsdp": peer}, device_id_type=MESH)

    for d in range(1, n_fsdp):
        tok_copy(d, f, lax.rem(f + d, n_fsdp)).start()
    load_gate_up(1)
    own_copy.wait()
    for d in range(1, n_fsdp):
        tok_copy(d, lax.rem(f + n_fsdp - d, n_fsdp), f).wait_recv()
    for p in range(n_fsdp):
        xf[p * rows:(p + 1) * rows, :] = slots[p].astype(jnp.float32)
    x[...] = xf[...].astype(x.dtype)
    acc[...] = jnp.zeros_like(acc)

    def when(cond, run):
        if cond is True:
            run()
        else:
            pl.when(cond)(run)

    def part_copy(s, d):
        peer = lax.rem(t + d, n_tp)
        return pltpu.make_async_remote_copy(
            part.at[s, peer], recv.at[s, d - 1], p_send.at[s, d - 1], p_recv.at[s, d - 1],
            device_id={"tp": peer}, device_id_type=MESH)

    def hid_copy(s, d, owner):
        return pltpu.make_async_remote_copy(
            hid.at[s, owner], hid.at[s, owner], h_send.at[s, d - 1], h_recv.at[s, d - 1],
            device_id={"tp": lax.rem(t + d, n_tp)}, device_id_type=MESH)

    def load_ahead(s):
        if isinstance(s, int):
            load_down(2)
            load_down(3)
            return

        @pl.when(s + 2 < full)
        def _():
            load_gate_up(s + 2)

        @pl.when(s == full - 2)
        def _():
            if last_owners:
                load_gate_up(full)
            else:
                load_down(2)

        @pl.when(s == full - 1)
        def _():
            load_down(0)
            load_down(1)
            if not last_owners:
                load_down(3)

    def load_down_ahead(s):
        if isinstance(s, int):
            return

        @pl.when(s + 4 < full)
        def _():
            load_down(s + 4)

        if last_owners:
            @pl.when(s + 4 == full)
            def _():
                load_down(full)

    def gate_up(s, owners):
        size = owners * GROUP
        at = pl.ds(pl.multiple_of(s * chunk, chunk), size)
        for k, (source, target) in enumerate(((gate_w, wg), (up_w, wu))):
            pltpu.make_async_copy(source.at[at], target.at[at], w_sem.at[k, s]).wait()
        load_ahead(s)
        for k, target in enumerate((wg, wu)):
            sums = lax.dot_general(x[...], target[at, :], NT, preferred_element_type=jnp.float32)
            for j in range(owners):
                piece = sums[:, j * GROUP:(j + 1) * GROUP]
                part[s, j, k] = piece.astype(part.dtype)

                @pl.when(t == j)
                def _():
                    own[s, k] = piece
        for d in range(1, n_tp):
            when(True if owners == n_tp else lax.rem(t + d, n_tp) < owners,
                 lambda d=d: part_copy(s, d).start())

    def activate(s, owners):
        def run():
            gate, up = own[s, 0], own[s, 1]
            for d in range(1, n_tp):
                part_copy(s, d).wait_recv()
                gate = gate + recv[s, d - 1, 0].astype(jnp.float32)
                up = up + recv[s, d - 1, 1].astype(jnp.float32)
            hid[s, t] = (gate / (1.0 + jnp.exp(-gate)) * up).astype(hid.dtype)
            for d in range(1, n_tp):
                hid_copy(s, d, t).start()
        when(True if owners == n_tp else t < owners, run)

    def down(s, owners):
        size = owners * GROUP
        at = pl.ds(pl.multiple_of(s * chunk, chunk), size)
        for d in range(1, n_tp):
            owner = lax.rem(t + n_tp - d, n_tp)
            when(True if owners == n_tp else owner < owners,
                 lambda d=d, owner=owner: hid_copy(s, d, owner).wait_recv())
        pltpu.make_async_copy(down_w.at[at], wd.at[at], w_sem.at[2, s]).wait()
        load_down_ahead(s)
        h = jnp.concatenate([hid[s, j] for j in range(owners)], axis=1)
        acc[...] += jnp.dot(h, wd[at, :], preferred_element_type=jnp.float32)

    @pl.loop(0, full)
    def _(s):
        gate_up(s, n_tp)

        @pl.when(s >= LAG)
        def _():
            activate(s - LAG, n_tp)

    if last_owners:
        gate_up(full, last_owners)

    @pl.loop(full - LAG, full)
    def _(s):
        activate(s, n_tp)

    early = min(2, full)

    @pl.loop(0, early)
    def _(s):
        down(s, n_tp)

    if last_owners:
        activate(full, last_owners)

    @pl.loop(early, full)
    def _(s):
        down(s, n_tp)

    if last_owners:
        down(full, last_owners)

    def out_copy(d, peer):
        return pltpu.make_async_remote_copy(
            send.at[peer], land.at[d - 1], o_send.at[d - 1], o_recv.at[d - 1],
            device_id={"fsdp": peer}, device_id_type=MESH)

    for p in range(n_fsdp):
        send[p] = acc[p * rows:(p + 1) * rows, :]
    for d in range(1, n_fsdp):
        out_copy(d, lax.rem(f + d, n_fsdp)).start()
    total = send[f]
    for d in range(1, n_fsdp):
        out_copy(d, f).wait_recv()
        total = total + land[d - 1]
    out[...] = total

    for d in range(1, n_fsdp):
        tok_copy(d, f, f).wait_send()
        out_copy(d, f).wait_send()

    @pl.loop(0, full)
    def _(s):
        for d in range(1, n_tp):
            part_copy(s, d).wait_send()
            hid_copy(s, d, t).wait_send()

    if last_owners:
        for d in range(1, n_tp):
            when(lax.rem(t + d, n_tp) < last_owners, lambda d=d: part_copy(full, d).wait_send())
            when(t < last_owners, lambda d=d: hid_copy(full, d, t).wait_send())


def fused_call(n_fsdp, n_tp, tokens, gate_w, up_w, down_w):
    rows, width = tokens.shape
    hidden = gate_w.shape[0]
    chunks = -(-hidden // (GROUP * n_tp))
    every = rows * n_fsdp
    dma = pltpu.SemaphoreType.DMA
    any_spec = pl.BlockSpec(memory_space=pl.ANY)
    return pl.pallas_call(
        functools.partial(fused, n_fsdp, n_tp),
        out_shape=jax.ShapeDtypeStruct((rows, width), jnp.float32),
        in_specs=[any_spec] * 4,
        out_specs=pl.BlockSpec(memory_space=pltpu.VMEM),
        scratch_shapes=[
            pltpu.VMEM((hidden, width), gate_w.dtype),
            pltpu.VMEM((hidden, width), up_w.dtype),
            pltpu.VMEM((hidden, width), down_w.dtype),
            pltpu.VMEM((n_fsdp, rows, width), tokens.dtype),
            pltpu.VMEM((every, width), jnp.float32),
            pltpu.VMEM((every, width), tokens.dtype),
            pltpu.VMEM((chunks, n_tp, 2, every, GROUP), WIRE),
            pltpu.VMEM((chunks, 2, every, GROUP), jnp.float32),
            pltpu.VMEM((chunks, n_tp - 1, 2, every, GROUP), WIRE),
            pltpu.VMEM((chunks, n_tp, every, GROUP), jnp.bfloat16),
            pltpu.VMEM((every, width), jnp.float32),
            pltpu.VMEM((n_fsdp, rows, width), jnp.float32),
            pltpu.VMEM((n_fsdp - 1, rows, width), jnp.float32),
            dma((3, chunks)),
            dma,
            dma((n_fsdp - 1,)),
            dma((n_fsdp - 1,)),
            dma((chunks, n_tp - 1)),
            dma((chunks, n_tp - 1)),
            dma((chunks, n_tp - 1)),
            dma((chunks, n_tp - 1)),
            dma((n_fsdp - 1,)),
            dma((n_fsdp - 1,)),
        ],
        compiler_params=pltpu.CompilerParams(
            collective_id=0, has_side_effects=True, vmem_limit_bytes=VMEM_BYTES),
        cost_estimate=pl.CostEstimate(
            flops=6 * every * hidden * width, bytes_accessed=6 * hidden * width,
            transcendentals=every * hidden // n_tp),
        name="swiglu",
    )(tokens, gate_w, up_w, down_w).astype(tokens.dtype)


def collective_body(tokens, gate_weight, up_weight, down_weight):
    hidden_width = gate_weight.shape[0]
    block_rows = lax.all_gather(tokens, "fsdp", axis=0, tiled=True)
    gate_part = lax.dot_general(block_rows, gate_weight, NT, preferred_element_type=jnp.float32)
    up_part = lax.dot_general(block_rows, up_weight, NT, preferred_element_type=jnp.float32)
    partial_value = jnp.concatenate([gate_part, up_part], axis=1)
    share_rows = lax.psum_scatter(partial_value, "tp", scatter_dimension=0, tiled=True)
    quarter = (jax.nn.silu(share_rows[:, :hidden_width]) * share_rows[:, hidden_width:]).astype(
        jnp.bfloat16
    )
    hidden = lax.all_gather(quarter, "tp", axis=0, tiled=True)
    down_terms = jnp.dot(hidden, down_weight, preferred_element_type=jnp.float32)
    mixed = lax.psum_scatter(down_terms, "fsdp", scatter_dimension=0, tiled=True)
    return mixed.astype(jnp.bfloat16)


def solution(mesh):
    n_fsdp, n_tp = mesh.shape["fsdp"], mesh.shape["tp"]

    def body(tokens, gate_weight, up_weight, down_weight):
        hidden, width = gate_weight.shape
        every = tokens.shape[0] * n_fsdp
        resident = 6 * hidden * width + 24 * every * width + 48 * every * hidden
        if hidden % GROUP or hidden < GROUP * n_tp * 4 or every % 16 or resident > VMEM_BYTES:
            return collective_body(tokens, gate_weight, up_weight, down_weight)
        return fused_call(n_fsdp, n_tp, tokens, gate_weight, up_weight, down_weight)

    placed = (P("fsdp", "tp"),) * 4
    return jax.shard_map(
        body, mesh=mesh, in_specs=placed, out_specs=P("fsdp", "tp"), check_vma=False
    )
```

```python
import functools

import jax
import jax.numpy as jnp
from jax import lax
from jax.experimental import pallas as pl
from jax.experimental.pallas import tpu as pltpu
from jax.sharding import PartitionSpec as P

MESH = pl.DeviceIdType.MESH
GROUP = 128
LAG = 3
WIRE = jnp.float32
NT = (((1,), (1,)), ((), ()))
VMEM_BYTES = 58 * 2**20


def fused(n_fsdp, n_tp, tokens, gate_w, up_w, down_w, out,
          wg, wu, wd, slots, xf, x, part, own, recv, hid, acc, send, land,
          w_sem, own_sem, tok_send, tok_recv, p_send, p_recv, h_send, h_recv, o_send, o_recv):
    f, t = lax.axis_index("fsdp"), lax.axis_index("tp")
    rows, hidden = tokens.shape[0], gate_w.shape[0]
    chunk = GROUP * n_tp
    n_chunks = -(-hidden // chunk)
    full = hidden // chunk
    last_owners = (hidden - full * chunk) // GROUP

    def width(s):
        return min(chunk, hidden - s * chunk)

    def load(k, source, target, s):
        size = chunk if not isinstance(s, int) else width(s)
        at = pl.ds(s * chunk if isinstance(s, int) else pl.multiple_of(s * chunk, chunk), size)
        return pltpu.make_async_copy(source.at[at], target.at[at], w_sem.at[k, s])

    def start(k, s):
        source, target = ((gate_w, wg), (up_w, wu), (down_w, wd))[k]
        load(k, source, target, s).start(priority=1)

    start(0, 0)
    start(1, 0)
    own_copy = pltpu.make_async_copy(tokens, slots.at[f], own_sem)
    own_copy.start()

    barrier = pltpu.get_barrier_semaphore()
    for d in range(1, n_fsdp):
        pl.semaphore_signal(barrier, inc=1, device_id={"fsdp": lax.rem(f + d, n_fsdp)}, device_id_type=MESH)
    for d in range(1, n_tp):
        pl.semaphore_signal(barrier, inc=1, device_id={"tp": lax.rem(t + d, n_tp)}, device_id_type=MESH)
    pl.semaphore_wait(barrier, n_fsdp + n_tp - 2)

    def tok_copy(d, slot, peer):
        return pltpu.make_async_remote_copy(
            tokens, slots.at[slot], tok_send.at[d - 1], tok_recv.at[d - 1],
            device_id={"fsdp": peer}, device_id_type=MESH)

    for d in range(1, n_fsdp):
        tok_copy(d, f, lax.rem(f + d, n_fsdp)).start()
    own_copy.wait()
    for d in range(1, n_fsdp):
        tok_copy(d, lax.rem(f + n_fsdp - d, n_fsdp), f).wait_recv()
    for p in range(n_fsdp):
        xf[p * rows:(p + 1) * rows, :] = slots[p].astype(jnp.float32)
    x[...] = xf[...].astype(x.dtype)
    acc[...] = jnp.zeros_like(acc)

    def when(cond, run):
        if cond is True:
            run()
        else:
            pl.when(cond)(run)

    def part_copy(s, d):
        peer = lax.rem(t + d, n_tp)
        return pltpu.make_async_remote_copy(
            part.at[s, peer], recv.at[s, d - 1], p_send.at[s, d - 1], p_recv.at[s, d - 1],
            device_id={"tp": peer}, device_id_type=MESH)

    def hid_copy(s, d, owner):
        return pltpu.make_async_remote_copy(
            hid.at[s, owner], hid.at[s, owner], h_send.at[s, d - 1], h_recv.at[s, d - 1],
            device_id={"tp": lax.rem(t + d, n_tp)}, device_id_type=MESH)

    def start_next(k, s):
        if isinstance(s, int):
            start(2, k)
            return

        @pl.when(s + 1 < full)
        def _():
            start(k, s + 1)

        @pl.when(s + 1 == full)
        def _():
            if last_owners:
                start(k, full)
            else:
                start(2, k)

    def gate_up(s, owners):
        size = owners * GROUP
        at = pl.ds(pl.multiple_of(s * chunk, chunk), size)
        for k, (source, target) in enumerate(((gate_w, wg), (up_w, wu))):
            pltpu.make_async_copy(source.at[at], target.at[at], w_sem.at[k, s]).wait()
            start_next(k, s)
            sums = lax.dot_general(x[...], target[at, :], NT, preferred_element_type=jnp.float32)
            for j in range(owners):
                piece = sums[:, j * GROUP:(j + 1) * GROUP]
                part[s, j, k] = piece.astype(part.dtype)

                @pl.when(t == j)
                def _():
                    own[s, k] = piece
        for d in range(1, n_tp):
            when(True if owners == n_tp else lax.rem(t + d, n_tp) < owners,
                 lambda d=d: part_copy(s, d).start())

    def activate(s, owners):
        def run():
            gate, up = own[s, 0], own[s, 1]
            for d in range(1, n_tp):
                part_copy(s, d).wait_recv()
                gate = gate + recv[s, d - 1, 0].astype(jnp.float32)
                up = up + recv[s, d - 1, 1].astype(jnp.float32)
            hid[s, t] = (gate / (1.0 + jnp.exp(-gate)) * up).astype(hid.dtype)
            for d in range(1, n_tp):
                hid_copy(s, d, t).start()
        when(True if owners == n_tp else t < owners, run)

    def down(s, owners):
        size = owners * GROUP
        at = pl.ds(pl.multiple_of(s * chunk, chunk), size)
        for d in range(1, n_tp):
            owner = lax.rem(t + n_tp - d, n_tp)
            when(True if owners == n_tp else owner < owners,
                 lambda d=d, owner=owner: hid_copy(s, d, owner).wait_recv())
        pltpu.make_async_copy(down_w.at[at], wd.at[at], w_sem.at[2, s]).wait()
        h = jnp.concatenate([hid[s, j] for j in range(owners)], axis=1)
        acc[...] += jnp.dot(h, wd[at, :], preferred_element_type=jnp.float32)

    @pl.loop(0, full)
    def _(s):
        gate_up(s, n_tp)

        @pl.when(s >= LAG)
        def _():
            activate(s - LAG, n_tp)

    if last_owners:
        gate_up(full, last_owners)

    for s in range(LAG):
        activate(full - LAG + s, n_tp)
        start(2, s + 2)
        if s:
            down(s - 1, n_tp)
    if last_owners:
        activate(full, last_owners)
    for s in range(LAG + 2, n_chunks):
        start(2, s)

    @pl.loop(LAG - 1, full)
    def _(s):
        down(s, n_tp)

    if last_owners:
        down(full, last_owners)

    def out_copy(d, peer):
        return pltpu.make_async_remote_copy(
            send.at[peer], land.at[d - 1], o_send.at[d - 1], o_recv.at[d - 1],
            device_id={"fsdp": peer}, device_id_type=MESH)

    for p in range(n_fsdp):
        send[p] = acc[p * rows:(p + 1) * rows, :]
    for d in range(1, n_fsdp):
        out_copy(d, lax.rem(f + d, n_fsdp)).start()
    total = send[f]
    for d in range(1, n_fsdp):
        out_copy(d, f).wait_recv()
        total = total + land[d - 1]
    out[...] = total

    for d in range(1, n_fsdp):
        tok_copy(d, f, f).wait_send()
        out_copy(d, f).wait_send()

    @pl.loop(0, full)
    def _(s):
        for d in range(1, n_tp):
            part_copy(s, d).wait_send()
            hid_copy(s, d, t).wait_send()

    if last_owners:
        for d in range(1, n_tp):
            when(lax.rem(t + d, n_tp) < last_owners, lambda d=d: part_copy(full, d).wait_send())
            when(t < last_owners, lambda d=d: hid_copy(full, d, t).wait_send())


def fused_call(n_fsdp, n_tp, tokens, gate_w, up_w, down_w):
    rows, width = tokens.shape
    hidden = gate_w.shape[0]
    chunks = -(-hidden // (GROUP * n_tp))
    every = rows * n_fsdp
    dma = pltpu.SemaphoreType.DMA
    any_spec = pl.BlockSpec(memory_space=pl.ANY)
    return pl.pallas_call(
        functools.partial(fused, n_fsdp, n_tp),
        out_shape=jax.ShapeDtypeStruct((rows, width), jnp.float32),
        in_specs=[any_spec] * 4,
        out_specs=pl.BlockSpec(memory_space=pltpu.VMEM),
        scratch_shapes=[
            pltpu.VMEM((hidden, width), gate_w.dtype),
            pltpu.VMEM((hidden, width), up_w.dtype),
            pltpu.VMEM((hidden, width), down_w.dtype),
            pltpu.VMEM((n_fsdp, rows, width), tokens.dtype),
            pltpu.VMEM((every, width), jnp.float32),
            pltpu.VMEM((every, width), tokens.dtype),
            pltpu.VMEM((chunks, n_tp, 2, every, GROUP), WIRE),
            pltpu.VMEM((chunks, 2, every, GROUP), jnp.float32),
            pltpu.VMEM((chunks, n_tp - 1, 2, every, GROUP), WIRE),
            pltpu.VMEM((chunks, n_tp, every, GROUP), jnp.bfloat16),
            pltpu.VMEM((every, width), jnp.float32),
            pltpu.VMEM((n_fsdp, rows, width), jnp.float32),
            pltpu.VMEM((n_fsdp - 1, rows, width), jnp.float32),
            dma((3, chunks)),
            dma,
            dma((n_fsdp - 1,)),
            dma((n_fsdp - 1,)),
            dma((chunks, n_tp - 1)),
            dma((chunks, n_tp - 1)),
            dma((chunks, n_tp - 1)),
            dma((chunks, n_tp - 1)),
            dma((n_fsdp - 1,)),
            dma((n_fsdp - 1,)),
        ],
        compiler_params=pltpu.CompilerParams(
            collective_id=0, has_side_effects=True, vmem_limit_bytes=VMEM_BYTES),
        cost_estimate=pl.CostEstimate(
            flops=6 * every * hidden * width, bytes_accessed=6 * hidden * width,
            transcendentals=every * hidden // n_tp),
        name="swiglu",
    )(tokens, gate_w, up_w, down_w).astype(tokens.dtype)


def collective_body(tokens, gate_weight, up_weight, down_weight):
    hidden_width = gate_weight.shape[0]
    block_rows = lax.all_gather(tokens, "fsdp", axis=0, tiled=True)
    gate_part = lax.dot_general(block_rows, gate_weight, NT, preferred_element_type=jnp.float32)
    up_part = lax.dot_general(block_rows, up_weight, NT, preferred_element_type=jnp.float32)
    partial_value = jnp.concatenate([gate_part, up_part], axis=1)
    share_rows = lax.psum_scatter(partial_value, "tp", scatter_dimension=0, tiled=True)
    quarter = (jax.nn.silu(share_rows[:, :hidden_width]) * share_rows[:, hidden_width:]).astype(
        jnp.bfloat16
    )
    hidden = lax.all_gather(quarter, "tp", axis=0, tiled=True)
    down_terms = jnp.dot(hidden, down_weight, preferred_element_type=jnp.float32)
    mixed = lax.psum_scatter(down_terms, "fsdp", scatter_dimension=0, tiled=True)
    return mixed.astype(jnp.bfloat16)


def solution(mesh):
    n_fsdp, n_tp = mesh.shape["fsdp"], mesh.shape["tp"]

    def body(tokens, gate_weight, up_weight, down_weight):
        hidden, width = gate_weight.shape
        every = tokens.shape[0] * n_fsdp
        resident = 6 * hidden * width + 24 * every * width + 48 * every * hidden
        if hidden % GROUP or hidden < GROUP * n_tp * (LAG + 2) or every % 16 or resident > VMEM_BYTES:
            return collective_body(tokens, gate_weight, up_weight, down_weight)
        return fused_call(n_fsdp, n_tp, tokens, gate_weight, up_weight, down_weight)

    placed = (P("fsdp", "tp"),) * 4
    return jax.shard_map(
        body, mesh=mesh, in_specs=placed, out_specs=P("fsdp", "tp"), check_vma=False
    )
```

```python
import functools

import jax
import jax.numpy as jnp
from jax import lax
from jax.experimental import pallas as pl
from jax.experimental.pallas import tpu as pltpu
from jax.sharding import PartitionSpec as P

MESH = pl.DeviceIdType.MESH
GROUP = 128
LAG = 3
OUT_PARTS = 2
AHEAD = 4
NT = (((1,), (1,)), ((), ()))
VMEM_BYTES = 58 * 2**20


def fused(n_fsdp, n_tp, tokens, gate_w, up_w, down_w, out,
          wg, wu, wd, slots, xf, x, part, recv, hid, acc, send, land,
          w_sem, own_sem, tok_send, tok_recv, p_send, p_recv, h_send, h_recv, o_send, o_recv):
    f, t = lax.axis_index("fsdp"), lax.axis_index("tp")
    (rows, whole), hidden = tokens.shape, gate_w.shape[0]
    part_width = whole // OUT_PARTS
    chunk = GROUP * n_tp
    n_chunks = -(-hidden // chunk)
    full = hidden // chunk
    last_owners = (hidden - full * chunk) // GROUP

    def width(s):
        return min(chunk, hidden - s * chunk)

    def load(k, source, target, s):
        size = chunk if not isinstance(s, int) else width(s)
        at = pl.ds(s * chunk if isinstance(s, int) else pl.multiple_of(s * chunk, chunk), size)
        return pltpu.make_async_copy(source.at[at], target.at[at], w_sem.at[k, s])

    def start(k, s):
        source, target = ((gate_w, wg), (up_w, wu), (down_w, wd))[k]
        load(k, source, target, s).start(priority=1)

    def start_down(s):
        if isinstance(s, int):
            if s < n_chunks:
                start(2, s)
            return

        @pl.when(jnp.logical_and(s >= 0, s < full))
        def _():
            start(2, s)

        if last_owners:
            @pl.when(s == full)
            def _():
                start(2, full)

    start(0, 0)
    start(1, 0)
    own_copy = pltpu.make_async_copy(tokens, slots.at[f], own_sem)
    own_copy.start()

    barrier = pltpu.get_barrier_semaphore()
    for d in range(1, n_fsdp):
        pl.semaphore_signal(barrier, inc=1, device_id={"fsdp": lax.rem(f + d, n_fsdp)}, device_id_type=MESH)
    for d in range(1, n_tp):
        pl.semaphore_signal(barrier, inc=1, device_id={"tp": lax.rem(t + d, n_tp)}, device_id_type=MESH)
    pl.semaphore_wait(barrier, n_fsdp + n_tp - 2)

    def tok_copy(d, slot, peer):
        return pltpu.make_async_remote_copy(
            tokens, slots.at[slot], tok_send.at[d - 1], tok_recv.at[d - 1],
            device_id={"fsdp": peer}, device_id_type=MESH)

    for d in range(1, n_fsdp):
        tok_copy(d, f, lax.rem(f + d, n_fsdp)).start()
    for s in range(1, AHEAD):
        start(0, s)
        start(1, s)
    own_copy.wait()
    for d in range(1, n_fsdp):
        tok_copy(d, lax.rem(f + n_fsdp - d, n_fsdp), f).wait_recv()
    for p in range(n_fsdp):
        xf[p * rows:(p + 1) * rows, :] = slots[p].astype(jnp.float32)
    x[...] = xf[...].astype(x.dtype)
    acc[...] = jnp.zeros_like(acc)

    def when(cond, run):
        if cond is True:
            run()
        else:
            pl.when(cond)(run)

    def part_copy(s, d):
        peer = lax.rem(t + d, n_tp)
        return pltpu.make_async_remote_copy(
            part.at[s, peer], recv.at[s, d - 1], p_send.at[s, d - 1], p_recv.at[s, d - 1],
            device_id={"tp": peer}, device_id_type=MESH)

    def hid_copy(s, d, owner):
        return pltpu.make_async_remote_copy(
            hid.at[s, owner], hid.at[s, owner], h_send.at[s, d - 1], h_recv.at[s, d - 1],
            device_id={"tp": lax.rem(t + d, n_tp)}, device_id_type=MESH)

    def start_next(k, s):
        later = s + AHEAD
        if not isinstance(s, int):
            @pl.when(later < full)
            def _():
                start(k, later)

            if last_owners:
                @pl.when(later == full)
                def _():
                    start(k, full)
        start_down(2 * (later - n_chunks) + k)

    def gate_up(s, owners):
        size = owners * GROUP
        at = pl.ds(pl.multiple_of(s * chunk, chunk), size)
        for k, (source, target) in enumerate(((gate_w, wg), (up_w, wu))):
            pltpu.make_async_copy(source.at[at], target.at[at], w_sem.at[k, s]).wait()
            start_next(k, s)
            sums = lax.dot_general(x[...], target[at, :], NT, preferred_element_type=jnp.float32)
            for j in range(owners):
                piece = sums[:, j * GROUP:(j + 1) * GROUP]
                part[s, j, k] = piece
        for d in range(1, n_tp):
            when(True if owners == n_tp else lax.rem(t + d, n_tp) < owners,
                 lambda d=d: part_copy(s, d).start())

    def activate(s, owners):
        def run():
            gate, up = part[s, t, 0], part[s, t, 1]
            for d in range(1, n_tp):
                part_copy(s, d).wait_recv()
                gate = gate + recv[s, d - 1, 0]
                up = up + recv[s, d - 1, 1]
            hid[s, t] = (gate / (1.0 + jnp.exp(-gate)) * up).astype(hid.dtype)
            for d in range(1, n_tp):
                hid_copy(s, d, t).start()
        when(True if owners == n_tp else t < owners, run)

    def arrive(s, owners):
        size = owners * GROUP
        at = pl.ds(pl.multiple_of(s * chunk, chunk), size)
        for d in range(1, n_tp):
            owner = lax.rem(t + n_tp - d, n_tp)
            when(True if owners == n_tp else owner < owners,
                 lambda d=d, owner=owner: hid_copy(s, d, owner).wait_recv())
        pltpu.make_async_copy(down_w.at[at], wd.at[at], w_sem.at[2, s]).wait()

    def down(s, owners, first, last):
        at = pl.ds(pl.multiple_of(s * chunk, chunk), owners * GROUP)
        h = jnp.concatenate([hid[s, j] for j in range(owners)], axis=1)
        acc[:, first:last] += jnp.dot(h, wd[at, first:last], preferred_element_type=jnp.float32)

    def out_copy(k, d, peer):
        return pltpu.make_async_remote_copy(
            send.at[k, peer], land.at[k, d - 1], o_send.at[k, d - 1], o_recv.at[k, d - 1],
            device_id={"fsdp": peer}, device_id_type=MESH)

    def send_out(k):
        for p in range(n_fsdp):
            send[k, p] = acc[p * rows:(p + 1) * rows, k * part_width:(k + 1) * part_width]
        for d in range(1, n_fsdp):
            out_copy(k, d, lax.rem(f + d, n_fsdp)).start()

    @pl.loop(0, full)
    def _(s):
        gate_up(s, n_tp)

        @pl.when(s >= LAG)
        def _():
            activate(s - LAG, n_tp)

    if last_owners:
        gate_up(full, last_owners)

    for s in range(2 * AHEAD, n_chunks):
        start_down(s)
    for s in range(LAG):
        activate(full - LAG + s, n_tp)
        if s:
            arrive(s - 1, n_tp)
            down(s - 1, n_tp, 0, whole)
    if last_owners:
        activate(full, last_owners)

    @pl.loop(LAG - 1, full - 1)
    def _(s):
        arrive(s, n_tp)
        down(s, n_tp, 0, whole)

    arrive(full - 1, n_tp)
    if last_owners:
        arrive(full, last_owners)
    for k in range(OUT_PARTS):
        down(full - 1, n_tp, k * part_width, (k + 1) * part_width)
        if last_owners:
            down(full, last_owners, k * part_width, (k + 1) * part_width)
        send_out(k)
    for k in range(OUT_PARTS):
        total = send[k, f]
        for d in range(1, n_fsdp):
            out_copy(k, d, f).wait_recv()
            total = total + land[k, d - 1]
        out[:, k * part_width:(k + 1) * part_width] = total

    for d in range(1, n_fsdp):
        tok_copy(d, f, f).wait_send()
        for k in range(OUT_PARTS):
            out_copy(k, d, f).wait_send()

    @pl.loop(0, full)
    def _(s):
        for d in range(1, n_tp):
            part_copy(s, d).wait_send()
            hid_copy(s, d, t).wait_send()

    if last_owners:
        for d in range(1, n_tp):
            when(lax.rem(t + d, n_tp) < last_owners, lambda d=d: part_copy(full, d).wait_send())
            when(t < last_owners, lambda d=d: hid_copy(full, d, t).wait_send())


def fused_call(n_fsdp, n_tp, tokens, gate_w, up_w, down_w):
    rows, width = tokens.shape
    hidden = gate_w.shape[0]
    chunks = -(-hidden // (GROUP * n_tp))
    every = rows * n_fsdp
    dma = pltpu.SemaphoreType.DMA
    any_spec = pl.BlockSpec(memory_space=pl.ANY)
    return pl.pallas_call(
        functools.partial(fused, n_fsdp, n_tp),
        out_shape=jax.ShapeDtypeStruct((rows, width), jnp.float32),
        in_specs=[any_spec] * 4,
        out_specs=pl.BlockSpec(memory_space=pltpu.VMEM),
        scratch_shapes=[
            pltpu.VMEM((hidden, width), gate_w.dtype),
            pltpu.VMEM((hidden, width), up_w.dtype),
            pltpu.VMEM((hidden, width), down_w.dtype),
            pltpu.VMEM((n_fsdp, rows, width), tokens.dtype),
            pltpu.VMEM((every, width), jnp.float32),
            pltpu.VMEM((every, width), tokens.dtype),
            pltpu.VMEM((chunks, n_tp, 2, every, GROUP), jnp.float32),
            pltpu.VMEM((chunks, n_tp - 1, 2, every, GROUP), jnp.float32),
            pltpu.VMEM((chunks, n_tp, every, GROUP), jnp.bfloat16),
            pltpu.VMEM((every, width), jnp.float32),
            pltpu.VMEM((OUT_PARTS, n_fsdp, rows, width // OUT_PARTS), jnp.float32),
            pltpu.VMEM((OUT_PARTS, n_fsdp - 1, rows, width // OUT_PARTS), jnp.float32),
            dma((3, chunks)),
            dma,
            dma((n_fsdp - 1,)),
            dma((n_fsdp - 1,)),
            dma((chunks, n_tp - 1)),
            dma((chunks, n_tp - 1)),
            dma((chunks, n_tp - 1)),
            dma((chunks, n_tp - 1)),
            dma((OUT_PARTS, n_fsdp - 1)),
            dma((OUT_PARTS, n_fsdp - 1)),
        ],
        compiler_params=pltpu.CompilerParams(
            collective_id=0, has_side_effects=True, vmem_limit_bytes=VMEM_BYTES),
        cost_estimate=pl.CostEstimate(
            flops=6 * every * hidden * width, bytes_accessed=6 * hidden * width,
            transcendentals=every * hidden // n_tp),
        name="swiglu",
    )(tokens, gate_w, up_w, down_w).astype(tokens.dtype)


def collective_body(tokens, gate_weight, up_weight, down_weight):
    hidden_width = gate_weight.shape[0]
    block_rows = lax.all_gather(tokens, "fsdp", axis=0, tiled=True)
    gate_part = lax.dot_general(block_rows, gate_weight, NT, preferred_element_type=jnp.float32)
    up_part = lax.dot_general(block_rows, up_weight, NT, preferred_element_type=jnp.float32)
    partial_value = jnp.concatenate([gate_part, up_part], axis=1)
    share_rows = lax.psum_scatter(partial_value, "tp", scatter_dimension=0, tiled=True)
    quarter = (jax.nn.silu(share_rows[:, :hidden_width]) * share_rows[:, hidden_width:]).astype(
        jnp.bfloat16
    )
    hidden = lax.all_gather(quarter, "tp", axis=0, tiled=True)
    down_terms = jnp.dot(hidden, down_weight, preferred_element_type=jnp.float32)
    mixed = lax.psum_scatter(down_terms, "fsdp", scatter_dimension=0, tiled=True)
    return mixed.astype(jnp.bfloat16)


def solution(mesh):
    n_fsdp, n_tp = mesh.shape["fsdp"], mesh.shape["tp"]

    def body(tokens, gate_weight, up_weight, down_weight):
        hidden, width = gate_weight.shape
        every = tokens.shape[0] * n_fsdp
        resident = 6 * hidden * width + 24 * every * width + 48 * every * hidden
        if hidden % GROUP or hidden < GROUP * n_tp * (AHEAD + 2) or every % 16 or resident > VMEM_BYTES:
            return collective_body(tokens, gate_weight, up_weight, down_weight)
        return fused_call(n_fsdp, n_tp, tokens, gate_weight, up_weight, down_weight)

    placed = (P("fsdp", "tp"),) * 4
    return jax.shard_map(
        body, mesh=mesh, in_specs=placed, out_specs=P("fsdp", "tp"), check_vma=False
    )
```

```python
import functools

import jax
import jax.numpy as jnp
from jax import lax
from jax.experimental import pallas as pl
from jax.experimental.pallas import tpu as pltpu
from jax.sharding import PartitionSpec as P

MESH = pl.DeviceIdType.MESH
GROUP = 128
LAG = 3
OUT_PARTS = 2
AHEAD = 4
WIRE = jnp.bfloat16
NT = (((1,), (1,)), ((), ()))
VMEM_BYTES = 58 * 2**20


def fused(n_fsdp, n_tp, tokens, gate_w, up_w, down_w, out,
          wg, wu, wd, slots, xf, x, own, part, recv, hid, acc, send, land,
          w_sem, own_sem, tok_send, tok_recv, p_send, p_recv, h_send, h_recv, o_send, o_recv):
    f, t = lax.axis_index("fsdp"), lax.axis_index("tp")
    (rows, whole), hidden = tokens.shape, gate_w.shape[0]
    every = rows * n_fsdp
    part_width = whole // OUT_PARTS
    chunk = GROUP * n_tp
    n_chunks = -(-hidden // chunk)
    full = hidden // chunk
    last_owners = (hidden - full * chunk) // GROUP

    def width(s):
        return min(chunk, hidden - s * chunk)

    def load(k, source, target, s):
        size = chunk if not isinstance(s, int) else width(s)
        at = pl.ds(s * chunk if isinstance(s, int) else pl.multiple_of(s * chunk, chunk), size)
        return pltpu.make_async_copy(source.at[at], target.at[at], w_sem.at[k, s])

    def start(k, s):
        source, target = ((gate_w, wg), (up_w, wu), (down_w, wd))[k]
        load(k, source, target, s).start(priority=1)

    def start_down(s):
        if isinstance(s, int):
            if s < n_chunks:
                start(2, s)
            return

        @pl.when(jnp.logical_and(s >= 0, s < full))
        def _():
            start(2, s)

        if last_owners:
            @pl.when(s == full)
            def _():
                start(2, full)

    start(0, 0)
    start(1, 0)
    xf[...] = jnp.zeros_like(xf)
    own_copy = pltpu.make_async_copy(tokens, slots.at[f], own_sem)
    own_copy.start()

    barrier = pltpu.get_barrier_semaphore()
    for d in range(1, n_fsdp):
        pl.semaphore_signal(barrier, inc=1, device_id={"fsdp": lax.rem(f + d, n_fsdp)}, device_id_type=MESH)
    for d in range(1, n_tp):
        pl.semaphore_signal(barrier, inc=1, device_id={"tp": lax.rem(t + d, n_tp)}, device_id_type=MESH)
    pl.semaphore_wait(barrier, n_fsdp + n_tp - 2)

    def tok_copy(d, slot, peer):
        return pltpu.make_async_remote_copy(
            tokens, slots.at[slot], tok_send.at[d - 1], tok_recv.at[d - 1],
            device_id={"fsdp": peer}, device_id_type=MESH)

    for d in range(1, n_fsdp):
        tok_copy(d, f, lax.rem(f + d, n_fsdp)).start()
    for s in range(1, AHEAD):
        start(0, s)
        start(1, s)
    own_copy.wait()
    for d in range(1, n_fsdp):
        tok_copy(d, lax.rem(f + n_fsdp - d, n_fsdp), f).wait_recv()
    for p in range(n_fsdp):
        xf[p * rows:(p + 1) * rows, :] = slots[p].astype(jnp.float32)
    x[...] = xf[...].T.astype(x.dtype)
    acc[...] = jnp.zeros_like(acc)

    def when(cond, run):
        if cond is True:
            run()
        else:
            pl.when(cond)(run)

    def part_copy(s, d):
        peer = lax.rem(t + d, n_tp)
        return pltpu.make_async_remote_copy(
            part.at[s, peer], recv.at[s, d - 1], p_send.at[s, d - 1], p_recv.at[s, d - 1],
            device_id={"tp": peer}, device_id_type=MESH)

    def hid_copy(s, d, owner):
        return pltpu.make_async_remote_copy(
            hid.at[s, owner], hid.at[s, owner], h_send.at[s, d - 1], h_recv.at[s, d - 1],
            device_id={"tp": lax.rem(t + d, n_tp)}, device_id_type=MESH)

    def start_next(k, s):
        later = s + AHEAD
        if not isinstance(s, int):
            @pl.when(later < full)
            def _():
                start(k, later)

            if last_owners:
                @pl.when(later == full)
                def _():
                    start(k, full)
        start_down(2 * (later - n_chunks) + k)

    def gate_up(s, owners):
        size = owners * GROUP
        at = pl.ds(pl.multiple_of(s * chunk, chunk), size)
        for k, (source, target) in enumerate(((gate_w, wg), (up_w, wu))):
            pltpu.make_async_copy(source.at[at], target.at[at], w_sem.at[k, s]).wait()
            start_next(k, s)
            sums = jnp.dot(target[at, :], x[...], preferred_element_type=jnp.float32).T[:every]
            for j in range(owners):
                piece = sums[:, j * GROUP:(j + 1) * GROUP]
                own[s, j, k] = piece
                part[s, j, k] = piece.astype(part.dtype)
        for d in range(1, n_tp):
            when(True if owners == n_tp else lax.rem(t + d, n_tp) < owners,
                 lambda d=d: part_copy(s, d).start())

    def activate(s, owners):
        def run():
            gate, up = own[s, t, 0], own[s, t, 1]
            for d in range(1, n_tp):
                part_copy(s, d).wait_recv()
                gate = gate + recv[s, d - 1, 0].astype(jnp.float32)
                up = up + recv[s, d - 1, 1].astype(jnp.float32)
            hid[s, t] = (gate / (1.0 + jnp.exp(-gate)) * up).astype(hid.dtype)
            for d in range(1, n_tp):
                hid_copy(s, d, t).start()
        when(True if owners == n_tp else t < owners, run)

    def arrive(s, owners):
        size = owners * GROUP
        at = pl.ds(pl.multiple_of(s * chunk, chunk), size)
        for d in range(1, n_tp):
            owner = lax.rem(t + n_tp - d, n_tp)
            when(True if owners == n_tp else owner < owners,
                 lambda d=d, owner=owner: hid_copy(s, d, owner).wait_recv())
        pltpu.make_async_copy(down_w.at[at], wd.at[at], w_sem.at[2, s]).wait()

    def down(s, owners, first, last):
        at = pl.ds(pl.multiple_of(s * chunk, chunk), owners * GROUP)
        h = jnp.concatenate([hid[s, j] for j in range(owners)], axis=1)
        acc[:, first:last] += jnp.dot(h, wd[at, first:last], preferred_element_type=jnp.float32)

    def out_copy(k, d, peer):
        return pltpu.make_async_remote_copy(
            send.at[k, peer], land.at[k, d - 1], o_send.at[k, d - 1], o_recv.at[k, d - 1],
            device_id={"fsdp": peer}, device_id_type=MESH)

    def send_out(k):
        for p in range(n_fsdp):
            send[k, p] = acc[p * rows:(p + 1) * rows, k * part_width:(k + 1) * part_width]
        for d in range(1, n_fsdp):
            out_copy(k, d, lax.rem(f + d, n_fsdp)).start()

    @pl.loop(0, full)
    def _(s):
        gate_up(s, n_tp)

        @pl.when(s >= LAG)
        def _():
            activate(s - LAG, n_tp)

    if last_owners:
        gate_up(full, last_owners)

    for s in range(2 * AHEAD, n_chunks):
        start_down(s)
    for s in range(LAG):
        activate(full - LAG + s, n_tp)
        if s:
            arrive(s - 1, n_tp)
            down(s - 1, n_tp, 0, whole)
    if last_owners:
        activate(full, last_owners)

    @pl.loop(LAG - 1, full - 1)
    def _(s):
        arrive(s, n_tp)
        down(s, n_tp, 0, whole)

    arrive(full - 1, n_tp)
    if last_owners:
        arrive(full, last_owners)
    for k in range(OUT_PARTS):
        down(full - 1, n_tp, k * part_width, (k + 1) * part_width)
        if last_owners:
            down(full, last_owners, k * part_width, (k + 1) * part_width)
        send_out(k)
    for k in range(OUT_PARTS):
        total = send[k, f]
        for d in range(1, n_fsdp):
            out_copy(k, d, f).wait_recv()
            total = total + land[k, d - 1]
        out[:, k * part_width:(k + 1) * part_width] = total

    for d in range(1, n_fsdp):
        tok_copy(d, f, f).wait_send()
        for k in range(OUT_PARTS):
            out_copy(k, d, f).wait_send()

    @pl.loop(0, full)
    def _(s):
        for d in range(1, n_tp):
            part_copy(s, d).wait_send()
            hid_copy(s, d, t).wait_send()

    if last_owners:
        for d in range(1, n_tp):
            when(lax.rem(t + d, n_tp) < last_owners, lambda d=d: part_copy(full, d).wait_send())
            when(t < last_owners, lambda d=d: hid_copy(full, d, t).wait_send())


def fused_call(n_fsdp, n_tp, tokens, gate_w, up_w, down_w):
    rows, width = tokens.shape
    hidden = gate_w.shape[0]
    chunks = -(-hidden // (GROUP * n_tp))
    every = rows * n_fsdp
    dma = pltpu.SemaphoreType.DMA
    any_spec = pl.BlockSpec(memory_space=pl.ANY)
    return pl.pallas_call(
        functools.partial(fused, n_fsdp, n_tp),
        out_shape=jax.ShapeDtypeStruct((rows, width), jnp.float32),
        in_specs=[any_spec] * 4,
        out_specs=pl.BlockSpec(memory_space=pltpu.VMEM),
        scratch_shapes=[
            pltpu.VMEM((hidden, width), gate_w.dtype),
            pltpu.VMEM((hidden, width), up_w.dtype),
            pltpu.VMEM((hidden, width), down_w.dtype),
            pltpu.VMEM((n_fsdp, rows, width), tokens.dtype),
            pltpu.VMEM((GROUP, width), jnp.float32),
            pltpu.VMEM((width, GROUP), tokens.dtype),
            pltpu.VMEM((chunks, n_tp, 2, every, GROUP), jnp.float32),
            pltpu.VMEM((chunks, n_tp, 2, every, GROUP), WIRE),
            pltpu.VMEM((chunks, n_tp - 1, 2, every, GROUP), WIRE),
            pltpu.VMEM((chunks, n_tp, every, GROUP), jnp.bfloat16),
            pltpu.VMEM((every, width), jnp.float32),
            pltpu.VMEM((OUT_PARTS, n_fsdp, rows, width // OUT_PARTS), jnp.float32),
            pltpu.VMEM((OUT_PARTS, n_fsdp - 1, rows, width // OUT_PARTS), jnp.float32),
            dma((3, chunks)),
            dma,
            dma((n_fsdp - 1,)),
            dma((n_fsdp - 1,)),
            dma((chunks, n_tp - 1)),
            dma((chunks, n_tp - 1)),
            dma((chunks, n_tp - 1)),
            dma((chunks, n_tp - 1)),
            dma((OUT_PARTS, n_fsdp - 1)),
            dma((OUT_PARTS, n_fsdp - 1)),
        ],
        compiler_params=pltpu.CompilerParams(
            collective_id=0, has_side_effects=True, vmem_limit_bytes=VMEM_BYTES),
        cost_estimate=pl.CostEstimate(
            flops=6 * every * hidden * width, bytes_accessed=6 * hidden * width,
            transcendentals=every * hidden // n_tp),
        name="swiglu",
    )(tokens, gate_w, up_w, down_w).astype(tokens.dtype)


def collective_body(tokens, gate_weight, up_weight, down_weight):
    hidden_width = gate_weight.shape[0]
    block_rows = lax.all_gather(tokens, "fsdp", axis=0, tiled=True)
    gate_part = lax.dot_general(block_rows, gate_weight, NT, preferred_element_type=jnp.float32)
    up_part = lax.dot_general(block_rows, up_weight, NT, preferred_element_type=jnp.float32)
    partial_value = jnp.concatenate([gate_part, up_part], axis=1)
    share_rows = lax.psum_scatter(partial_value, "tp", scatter_dimension=0, tiled=True)
    quarter = (jax.nn.silu(share_rows[:, :hidden_width]) * share_rows[:, hidden_width:]).astype(
        jnp.bfloat16
    )
    hidden = lax.all_gather(quarter, "tp", axis=0, tiled=True)
    down_terms = jnp.dot(hidden, down_weight, preferred_element_type=jnp.float32)
    mixed = lax.psum_scatter(down_terms, "fsdp", scatter_dimension=0, tiled=True)
    return mixed.astype(jnp.bfloat16)


def solution(mesh):
    n_fsdp, n_tp = mesh.shape["fsdp"], mesh.shape["tp"]

    def body(tokens, gate_weight, up_weight, down_weight):
        hidden, width = gate_weight.shape
        every = tokens.shape[0] * n_fsdp
        resident = 6 * hidden * width + 24 * every * width + 48 * every * hidden
        if hidden % GROUP or hidden < GROUP * n_tp * (AHEAD + 2) or every % 16 or every > GROUP or resident > VMEM_BYTES:
            return collective_body(tokens, gate_weight, up_weight, down_weight)
        return fused_call(n_fsdp, n_tp, tokens, gate_weight, up_weight, down_weight)

    placed = (P("fsdp", "tp"),) * 4
    return jax.shard_map(
        body, mesh=mesh, in_specs=placed, out_specs=P("fsdp", "tp"), check_vma=False
    )
```

```python
import functools

import jax
import jax.numpy as jnp
from jax import lax
from jax.experimental import pallas as pl
from jax.experimental.pallas import tpu as pltpu
from jax.sharding import PartitionSpec as P

MESH = pl.DeviceIdType.MESH
GROUP = 128
SPAN = 2
LAG = 4
OUT_PARTS = 2
AHEAD = 4
NT = (((1,), (1,)), ((), ()))
VMEM_BYTES = 58 * 2**20


def fused(n_fsdp, n_tp, tokens, gate_w, up_w, down_w, out,
          wg, wu, wd, slots, xf, x, part, recv, hid, acc, send, land,
          w_sem, own_sem, tok_send, tok_recv, p_send, p_recv, h_send, h_recv, o_send, o_recv):
    f, t = lax.axis_index("fsdp"), lax.axis_index("tp")
    (rows, whole), hidden = tokens.shape, gate_w.shape[0]
    part_width = whole // OUT_PARTS
    chunk = GROUP * n_tp
    n_chunks = -(-hidden // chunk)
    full = hidden // chunk
    last_owners = (hidden - full * chunk) // GROUP

    def width(s):
        return min(chunk, hidden - s * chunk)

    def load(k, source, target, s):
        size = chunk if not isinstance(s, int) else width(s)
        at = pl.ds(s * chunk if isinstance(s, int) else pl.multiple_of(s * chunk, chunk), size)
        return pltpu.make_async_copy(source.at[at], target.at[at], w_sem.at[k, s])

    def start(k, s):
        source, target = ((gate_w, wg), (up_w, wu), (down_w, wd))[k]
        load(k, source, target, s).start(priority=1)

    def start_down(s):
        if isinstance(s, int):
            if s < n_chunks:
                start(2, s)
            return

        @pl.when(jnp.logical_and(s >= 0, s < full))
        def _():
            start(2, s)

        if last_owners:
            @pl.when(s == full)
            def _():
                start(2, full)

    start(0, 0)
    start(1, 0)
    own_copy = pltpu.make_async_copy(tokens, slots.at[f], own_sem)
    own_copy.start()

    barrier = pltpu.get_barrier_semaphore()
    for d in range(1, n_fsdp):
        pl.semaphore_signal(barrier, inc=1, device_id={"fsdp": lax.rem(f + d, n_fsdp)}, device_id_type=MESH)
    for d in range(1, n_tp):
        pl.semaphore_signal(barrier, inc=1, device_id={"tp": lax.rem(t + d, n_tp)}, device_id_type=MESH)
    pl.semaphore_wait(barrier, n_fsdp + n_tp - 2)

    def tok_copy(d, slot, peer):
        return pltpu.make_async_remote_copy(
            tokens, slots.at[slot], tok_send.at[d - 1], tok_recv.at[d - 1],
            device_id={"fsdp": peer}, device_id_type=MESH)

    for d in range(1, n_fsdp):
        tok_copy(d, f, lax.rem(f + d, n_fsdp)).start()
    for s in range(1, AHEAD):
        start(0, s)
        start(1, s)
    own_copy.wait()
    for d in range(1, n_fsdp):
        tok_copy(d, lax.rem(f + n_fsdp - d, n_fsdp), f).wait_recv()
    for p in range(n_fsdp):
        xf[p * rows:(p + 1) * rows, :] = slots[p].astype(jnp.float32)
    x[...] = xf[...].astype(x.dtype)
    acc[...] = jnp.zeros_like(acc)

    def when(cond, run):
        if cond is True:
            run()
        else:
            pl.when(cond)(run)

    def part_copy(s, d):
        peer = lax.rem(t + d, n_tp)
        return pltpu.make_async_remote_copy(
            part.at[s, peer], recv.at[s, d - 1], p_send.at[s, d - 1], p_recv.at[s, d - 1],
            device_id={"tp": peer}, device_id_type=MESH)

    def hid_copy(s, d, owner):
        return pltpu.make_async_remote_copy(
            hid.at[s, owner], hid.at[s, owner], h_send.at[s, d - 1], h_recv.at[s, d - 1],
            device_id={"tp": lax.rem(t + d, n_tp)}, device_id_type=MESH)

    def start_next(k, s):
        later = s + AHEAD
        if not isinstance(s, int):
            @pl.when(later < full)
            def _():
                start(k, later)

            if last_owners:
                @pl.when(later == full)
                def _():
                    start(k, full)
        start_down(2 * (later - n_chunks) + k)

    def gate_up(chunks, owners):
        def at(s):
            return pl.ds(pl.multiple_of(s * chunk, chunk), owners * GROUP)

        for s in chunks:
            for k, (source, target) in enumerate(((gate_w, wg), (up_w, wu))):
                pltpu.make_async_copy(source.at[at(s)], target.at[at(s)], w_sem.at[k, s]).wait()
                start_next(k, s)
        sums = [[lax.dot_general(x[...], target[at(s), :], NT, preferred_element_type=jnp.float32)
                 for target in (wg, wu)] for s in chunks]
        for s, pair in zip(chunks, sums):
            for k in range(2):
                for j in range(owners):
                    part[s, j, k] = pair[k][:, j * GROUP:(j + 1) * GROUP]
        for s in chunks:
            for d in range(1, n_tp):
                when(True if owners == n_tp else lax.rem(t + d, n_tp) < owners,
                     lambda s=s, d=d: part_copy(s, d).start())

    def activate(s, owners):
        def run():
            gate, up = part[s, t, 0], part[s, t, 1]
            for d in range(1, n_tp):
                part_copy(s, d).wait_recv()
                gate = gate + recv[s, d - 1, 0]
                up = up + recv[s, d - 1, 1]
            hid[s, t] = (gate / (1.0 + jnp.exp(-gate)) * up).astype(hid.dtype)
            for d in range(1, n_tp):
                hid_copy(s, d, t).start()
        when(True if owners == n_tp else t < owners, run)

    def arrive(s, owners):
        size = owners * GROUP
        at = pl.ds(pl.multiple_of(s * chunk, chunk), size)
        for d in range(1, n_tp):
            owner = lax.rem(t + n_tp - d, n_tp)
            when(True if owners == n_tp else owner < owners,
                 lambda d=d, owner=owner: hid_copy(s, d, owner).wait_recv())
        pltpu.make_async_copy(down_w.at[at], wd.at[at], w_sem.at[2, s]).wait()

    def down(s, owners, first, last):
        at = pl.ds(pl.multiple_of(s * chunk, chunk), owners * GROUP)
        h = jnp.concatenate([hid[s, j] for j in range(owners)], axis=1)
        acc[:, first:last] += jnp.dot(h, wd[at, first:last], preferred_element_type=jnp.float32)

    def out_copy(k, d, peer):
        return pltpu.make_async_remote_copy(
            send.at[k, peer], land.at[k, d - 1], o_send.at[k, d - 1], o_recv.at[k, d - 1],
            device_id={"fsdp": peer}, device_id_type=MESH)

    def send_out(k):
        for p in range(n_fsdp):
            send[k, p] = acc[p * rows:(p + 1) * rows, k * part_width:(k + 1) * part_width]
        for d in range(1, n_fsdp):
            out_copy(k, d, lax.rem(f + d, n_fsdp)).start()

    @pl.loop(0, full // SPAN)
    def _(i):
        gate_up([i * SPAN + c for c in range(SPAN)], n_tp)

        @pl.when(i * SPAN >= LAG)
        def _():
            for c in range(SPAN):
                activate(i * SPAN + c - LAG, n_tp)

    if last_owners:
        gate_up([full], last_owners)

    for s in range(2 * AHEAD, n_chunks):
        start_down(s)
    for s in range(LAG):
        activate(full - LAG + s, n_tp)
        if s:
            arrive(s - 1, n_tp)
            down(s - 1, n_tp, 0, whole)
    if last_owners:
        activate(full, last_owners)

    @pl.loop(LAG - 1, full - 1)
    def _(s):
        arrive(s, n_tp)
        down(s, n_tp, 0, whole)

    arrive(full - 1, n_tp)
    if last_owners:
        arrive(full, last_owners)
    for k in range(OUT_PARTS):
        down(full - 1, n_tp, k * part_width, (k + 1) * part_width)
        if last_owners:
            down(full, last_owners, k * part_width, (k + 1) * part_width)
        send_out(k)
    for k in range(OUT_PARTS):
        total = send[k, f]
        for d in range(1, n_fsdp):
            out_copy(k, d, f).wait_recv()
            total = total + land[k, d - 1]
        out[:, k * part_width:(k + 1) * part_width] = total

    for d in range(1, n_fsdp):
        tok_copy(d, f, f).wait_send()
        for k in range(OUT_PARTS):
            out_copy(k, d, f).wait_send()

    @pl.loop(0, full)
    def _(s):
        for d in range(1, n_tp):
            part_copy(s, d).wait_send()
            hid_copy(s, d, t).wait_send()

    if last_owners:
        for d in range(1, n_tp):
            when(lax.rem(t + d, n_tp) < last_owners, lambda d=d: part_copy(full, d).wait_send())
            when(t < last_owners, lambda d=d: hid_copy(full, d, t).wait_send())


def fused_call(n_fsdp, n_tp, tokens, gate_w, up_w, down_w):
    rows, width = tokens.shape
    hidden = gate_w.shape[0]
    chunks = -(-hidden // (GROUP * n_tp))
    every = rows * n_fsdp
    dma = pltpu.SemaphoreType.DMA
    any_spec = pl.BlockSpec(memory_space=pl.ANY)
    return pl.pallas_call(
        functools.partial(fused, n_fsdp, n_tp),
        out_shape=jax.ShapeDtypeStruct((rows, width), jnp.float32),
        in_specs=[any_spec] * 4,
        out_specs=pl.BlockSpec(memory_space=pltpu.VMEM),
        scratch_shapes=[
            pltpu.VMEM((hidden, width), gate_w.dtype),
            pltpu.VMEM((hidden, width), up_w.dtype),
            pltpu.VMEM((hidden, width), down_w.dtype),
            pltpu.VMEM((n_fsdp, rows, width), tokens.dtype),
            pltpu.VMEM((every, width), jnp.float32),
            pltpu.VMEM((every, width), tokens.dtype),
            pltpu.VMEM((chunks, n_tp, 2, every, GROUP), jnp.float32),
            pltpu.VMEM((chunks, n_tp - 1, 2, every, GROUP), jnp.float32),
            pltpu.VMEM((chunks, n_tp, every, GROUP), jnp.bfloat16),
            pltpu.VMEM((every, width), jnp.float32),
            pltpu.VMEM((OUT_PARTS, n_fsdp, rows, width // OUT_PARTS), jnp.float32),
            pltpu.VMEM((OUT_PARTS, n_fsdp - 1, rows, width // OUT_PARTS), jnp.float32),
            dma((3, chunks)),
            dma,
            dma((n_fsdp - 1,)),
            dma((n_fsdp - 1,)),
            dma((chunks, n_tp - 1)),
            dma((chunks, n_tp - 1)),
            dma((chunks, n_tp - 1)),
            dma((chunks, n_tp - 1)),
            dma((OUT_PARTS, n_fsdp - 1)),
            dma((OUT_PARTS, n_fsdp - 1)),
        ],
        compiler_params=pltpu.CompilerParams(
            collective_id=0, has_side_effects=True, vmem_limit_bytes=VMEM_BYTES),
        cost_estimate=pl.CostEstimate(
            flops=6 * every * hidden * width, bytes_accessed=6 * hidden * width,
            transcendentals=every * hidden // n_tp),
        name="swiglu",
    )(tokens, gate_w, up_w, down_w).astype(tokens.dtype)


def collective_body(tokens, gate_weight, up_weight, down_weight):
    hidden_width = gate_weight.shape[0]
    block_rows = lax.all_gather(tokens, "fsdp", axis=0, tiled=True)
    gate_part = lax.dot_general(block_rows, gate_weight, NT, preferred_element_type=jnp.float32)
    up_part = lax.dot_general(block_rows, up_weight, NT, preferred_element_type=jnp.float32)
    partial_value = jnp.concatenate([gate_part, up_part], axis=1)
    share_rows = lax.psum_scatter(partial_value, "tp", scatter_dimension=0, tiled=True)
    quarter = (jax.nn.silu(share_rows[:, :hidden_width]) * share_rows[:, hidden_width:]).astype(
        jnp.bfloat16
    )
    hidden = lax.all_gather(quarter, "tp", axis=0, tiled=True)
    down_terms = jnp.dot(hidden, down_weight, preferred_element_type=jnp.float32)
    mixed = lax.psum_scatter(down_terms, "fsdp", scatter_dimension=0, tiled=True)
    return mixed.astype(jnp.bfloat16)


def solution(mesh):
    n_fsdp, n_tp = mesh.shape["fsdp"], mesh.shape["tp"]

    def body(tokens, gate_weight, up_weight, down_weight):
        hidden, width = gate_weight.shape
        every = tokens.shape[0] * n_fsdp
        resident = 6 * hidden * width + 24 * every * width + 48 * every * hidden
        if hidden % GROUP or hidden < GROUP * n_tp * (AHEAD + 2) or hidden // (GROUP * n_tp) % SPAN or every % 16 or resident > VMEM_BYTES:
            return collective_body(tokens, gate_weight, up_weight, down_weight)
        return fused_call(n_fsdp, n_tp, tokens, gate_weight, up_weight, down_weight)

    placed = (P("fsdp", "tp"),) * 4
    return jax.shard_map(
        body, mesh=mesh, in_specs=placed, out_specs=P("fsdp", "tp"), check_vma=False
    )
```
